512 devices in a mesh: tm: 16 (over x, y_hi, core), height: 16 (over z), mp: 2 (over y_lo).
Axes of the slice: x: 4, y: 4 (y_hi: 2, y_lo: 2; y = y_hi * 2 + y_lo), z: 16, core: 2. Of those that a mesh axis runs over, the one named last changes fastest.
Arguments:
- queries: bfloat16 [16, 16, 384, 1536], P('tm', 'height', None, 'mp'), may hold values from -6 to 6
- key_field: bfloat16 [16, 16, 384, 1536], P('tm', 'height', None, 'mp'), may hold values from -10 to 10
- value_field: bfloat16 [16, 16, 384, 1536], P('tm', 'height', None, 'mp'), may hold values from -6 to 6
- stream: bfloat16 [16, 16, 384, 3072], P('tm', 'height', None, 'mp'), may hold values from -3 to 3
- gate_scale: float32 [3072], P('mp'), may hold values from 0.5 to 1.5
- out_weight: bfloat16 [1536, 3072], P('height', 'mp'), may hold values from -0.15625 to 0.15625
- tile_lists: int32 [16, 16, 9], P('tm', 'height'), may hold values from -1 to 255, as said below
Outputs:
- block_out: bfloat16 [16, 16, 384, 3072], P('tm', 'height', None, 'mp')
The draws below stay inside these ranges and needn't reach their ends.
Inputs may be any that keep to these rules, and one draw needn't show every extreme that they name: `tile_lists`: entry e names tile (e // 16, e % 16). The list of tile (a, b) names distinct tiles in increasing order, followed by -1 entries; they are all tiles of a box whose first indices form a run within a - 1 to a + 1 inside the same video (same a // 16) and whose second indices form a run within b - 1 to b + 1 inside the same column tile (same b // 16), and the box holds tile (a, b). Some list names 9 tiles and some list holds -1.
All inputs are finite; a program needn't handle non-finite values.
Results may differ from the reference program's by a relative error of at most 0.0059.
Values may be sent and summed in bfloat16 or wider, within the bound.
A program may use at most 128 MiB of HBM per device.

```python
import math
import jax
import jax.numpy as jnp
from jax import lax

D = 3072
HEADS = 12
HD = 128
WIN = 9
TILE_FRAMES = 16
TILE_ROWS = 16
TOK = 384
GROUPS_TM = 16
GROUPS_H = 16


def paired_fields(key):
    base = jax.random.fold_in(key, 7)
    draw_keys = jax.random.split(base, 2)
    grid_shape = (GROUPS_TM, GROUPS_H, TOK, HEADS * HD)
    query_vals = jnp.clip(jax.random.normal(draw_keys[0], grid_shape, jnp.float32), -4.0, 4.0)
    key_vals = 2.5 * jnp.clip(jax.random.normal(draw_keys[1], grid_shape, jnp.float32), -4.0, 4.0)
    return (query_vals, key_vals)


def draw_queries(key, part):
    return paired_fields(key)[0].astype(jnp.bfloat16)


def draw_key_field(key, part):
    return paired_fields(key)[1].astype(jnp.bfloat16)


def draw_tile_lists(key, part):
    draw_keys = jax.random.split(jax.random.fold_in(key, 11), 4)
    grid_shape = (GROUPS_TM, GROUPS_H)
    lower_frame = jax.random.randint(draw_keys[0], grid_shape, 0, 2)
    upper_frame = jax.random.randint(draw_keys[1], grid_shape, 0, 2)
    lower_row = jax.random.randint(draw_keys[2], grid_shape, 0, 2)
    upper_row = jax.random.randint(draw_keys[3], grid_shape, 0, 2)
    group_ids = jnp.arange(GROUPS_TM, dtype=jnp.int32)[:, None]
    strip_ids = jnp.arange(GROUPS_H, dtype=jnp.int32)[None, :]
    frame_ids = group_ids % TILE_FRAMES
    row_ids = strip_ids % TILE_ROWS
    centre = (group_ids == GROUPS_TM // 2) | (strip_ids == GROUPS_H // 2)
    lower_frame = jnp.where(centre, 1, lower_frame)
    upper_frame = jnp.where(centre, 1, upper_frame)
    lower_row = jnp.where(centre, 1, lower_row)
    upper_row = jnp.where(centre, 1, upper_row)
    included_list = []
    tile_id_list = []
    for slot_frame in range(3):
        for slot_row in range(3):
            step_frame = slot_frame - 1
            step_row = slot_row - 1
            near_frame = frame_ids + step_frame
            near_row = row_ids + step_row
            included = (step_frame >= -lower_frame) & (step_frame <= upper_frame)
            included = included & (step_row >= -lower_row) & (step_row <= upper_row)
            included = included & (near_frame >= 0) & (near_frame < TILE_FRAMES)
            included = included & (near_row >= 0) & (near_row < TILE_ROWS)
            included_list.append(included)
            tile_id_list.append(jnp.broadcast_to((group_ids + step_frame) * GROUPS_H + strip_ids + step_row, grid_shape))
    included_all = jnp.stack(included_list, -1)
    tile_ids = jnp.stack(tile_id_list, -1)
    order_key = jnp.where(included_all, 0, 9) + jnp.arange(9, dtype=jnp.int32)
    ranked = jnp.argsort(order_key, axis=-1, stable=True)
    tile_ids = jnp.take_along_axis(tile_ids, ranked, axis=-1)
    included_all = jnp.take_along_axis(included_all, ranked, axis=-1)
    return jnp.where(included_all, tile_ids, -1).astype(jnp.int32)


def steps_of(stream_key, dims, cuts, low, high):
    loudness, own = 1.0, jax.random.fold_in(stream_key, 6)
    for position, shards_of in cuts:
        draws = jnp.exp(jax.random.uniform(jax.random.fold_in(own, position), (shards_of,), jnp.float32, low / len(cuts), high / len(cuts)))
        loudness = loudness * jnp.repeat(draws, dims[position] // shards_of).reshape([-1 if axis == position else 1 for axis in range(len(dims))])
    return loudness


def gaussian(rng, extent, deviation, reach, cuts=(), held_as=jnp.bfloat16):
    array = jax.random.normal(rng, extent, jnp.float32) * deviation
    if len(cuts) > 0:
        array = steps_of(rng, extent, cuts, -0.22, 0.18) * array
    return jnp.clip(array, min=-reach, max=reach).astype(held_as)


def setup_inputs(seed: int = 0) -> dict:
    key_of = jax.random.split(jax.random.key(seed), 8)
    queries = draw_queries(jax.random.fold_in(key_of[7], 71), 0)
    key_field = draw_key_field(jax.random.fold_in(key_of[7], 71), 0)
    value_field = gaussian(key_of[2], (GROUPS_TM, GROUPS_H, TOK, HEADS * HD), 1.0, 6.0, ((0, 16), (1, 16), (3, 2)))
    stream = gaussian(key_of[3], (GROUPS_TM, GROUPS_H, TOK, D), 0.5, 3.0, ((0, 16), (1, 16), (3, 2)))
    gate_scale = jnp.clip(0.5 + 1.0 * jax.random.uniform(key_of[4], (D,), jnp.float32) ** steps_of(key_of[4], (D,), ((0, 2),), -0.2, 0.2), 0.5, 1.5)
    out_weight = gaussian(key_of[5], (HEADS * HD, D), (HEADS * HD) ** -0.5, 0.15625, ((0, 16), (1, 2)))
    tile_lists = draw_tile_lists(jax.random.fold_in(key_of[7], 71), 0)
    return {"queries": queries, "key_field": key_field, "value_field": value_field, "stream": stream, "gate_scale": gate_scale, "out_weight": out_weight, "tile_lists": tile_lists}


def to_tiles(field):
    channels = field.shape[-1]
    return field.reshape(GROUPS_TM * GROUPS_H, TOK, channels)

def reference(queries, key_field, value_field, stream, gate_scale, out_weight, tile_lists):
    query_tiles = to_tiles(queries)
    key_tiles = to_tiles(key_field)
    value_tiles = to_tiles(value_field)
    tokens = TOK
    lists_flat = tile_lists.reshape(GROUPS_TM * GROUPS_H, WIN)
    score_scale = 1.0 / math.sqrt(HD)

    def one_tile(inputs):
        query_block, listed = inputs
        safe = jnp.maximum(listed, 0).astype(jnp.int32)
        key_block = key_tiles[safe].reshape(WIN * tokens, HEADS, HD).astype(jnp.float32)
        value_block = value_tiles[safe].reshape(WIN * tokens, HEADS, HD).astype(jnp.float32)
        key_mask = jnp.repeat(listed >= 0, tokens)
        query_three = query_block.reshape(tokens, HEADS, HD).astype(jnp.float32)
        scores = jnp.einsum('qhd,khd->hqk', query_three, key_block) * score_scale
        scores = jnp.where(key_mask[None, None, :], scores, -jnp.inf)
        row_max = lax.optimization_barrier(jnp.max(scores, axis=2, keepdims=True))
        weights = jnp.exp(scores - row_max).astype(jnp.bfloat16)
        total = lax.optimization_barrier(jnp.sum(weights.astype(jnp.float32), axis=2))
        summed = jnp.einsum('hqk,khd->hqd', weights.astype(jnp.float32), value_block)
        attended = summed / total[:, :, None]
        return attended.transpose(1, 0, 2).reshape(tokens, HEADS * HD).astype(jnp.bfloat16)
    attended = lax.map(one_tile, (query_tiles, lists_flat))
    attended = attended.reshape(GROUPS_TM * GROUPS_H * TOK, HEADS * HD)
    mixed = jnp.dot(attended, out_weight, preferred_element_type=jnp.float32)
    result = stream.reshape(GROUPS_TM * GROUPS_H * TOK, D).astype(jnp.float32) + gate_scale[None, :] * mixed
    return result.astype(jnp.bfloat16).reshape(stream.shape)
```

```python
import math

import jax
import jax.numpy as jnp
from jax import lax
from jax.experimental import pallas as pl
from jax.experimental.pallas import tpu as pltpu
from jax.sharding import PartitionSpec as P

HD = 128
TOK = 384
G = 3
HALF = 768
OUT = 1536
PIECE = 48
COLS = 384
SUB = 128
FAR = 1e30
MESH = pl.DeviceIdType.MESH


def attend(hh, qbuf, kbuf, vbuf, flags, osend):
    scale = math.log2(math.e) / math.sqrt(HD)

    def block(sub, carry):
        rows = pl.ds(pl.multiple_of(sub * SUB, SUB), SUB)
        for j in range(2):
            q = qbuf[hh, j, rows, :]
            scores, tops, biases = [], [], []
            for r in range(3):
                for dt in range(3):
                    keys = kbuf[hh, r, (j + dt) * TOK:(j + dt + 1) * TOK, :]
                    s = lax.dot_general(
                        q, keys, (((1,), (1,)), ((), ())), preferred_element_type=jnp.float32
                    )
                    bias = flags[j, r * 3 + dt:r * 3 + dt + 1, 0:1]
                    scores.append(s)
                    biases.append(bias)
                    tops.append(jnp.max(s, axis=1, keepdims=True) - bias)
            top = tops[0]
            for t in tops[1:]:
                top = jnp.maximum(top, t)
            total = jnp.zeros((SUB, 1), jnp.float32)
            acc = jnp.zeros((SUB, HD), jnp.float32)
            for n in range(9):
                r, dt = divmod(n, 3)
                shift = (top + biases[n]) * scale
                w = jnp.exp2(scores[n] * scale - shift)
                total = total + jnp.sum(w, axis=1, keepdims=True)
                values = vbuf[hh, r, (j + dt) * TOK:(j + dt + 1) * TOK, :]
                acc = acc + jnp.dot(
                    w.astype(jnp.bfloat16), values, preferred_element_type=jnp.float32
                )
            osend[hh, j, rows, :] = (acc / total).astype(jnp.bfloat16)
        return carry

    lax.fori_loop(0, TOK // SUB, block, 0)


def weight_rows(wbuf, xp, start, count):
    parts = []
    row = start
    while row < start + count:
        z, rest = divmod(row, 2 * PIECE)
        c, low = divmod(rest, PIECE)
        high = min(PIECE, low + start + count - row)
        parts.append(wbuf[xp, z, c, low:high, :])
        row += high - low
    return jnp.concatenate(parts, axis=0)


def project(hh, oall, wbuf, acc):
    left = oall[hh]
    for xp in range(4):
        right = jnp.concatenate(
            [weight_rows(wbuf, xp, (g * G + hh) * HD, HD) for g in range(4)], axis=0
        )
        part = jnp.dot(left, right, preferred_element_type=jnp.float32)
        cols = slice(xp * COLS, (xp + 1) * COLS)
        if hh == 0:
            acc[:, cols] = part
        else:
            acc[:, cols] += part


def finish(acc, stream, gate, out):
    out[0, 0] = (stream[...].astype(jnp.float32) + gate[...] * acc[...]).astype(jnp.bfloat16)


def kernel(
    q_in, k_in, v_in, stream_in, gate, w_in, lists, out,
    qbuf, kbuf, vbuf, mine, flags, osend, oall, wbuf, stream, acc,
    ys, yr, zs, zr, qs, qr, os_, or_, fs, fr, wzs, wzr, wxs, wxr, wss, wsr, ls,
):
    tm, h, m = lax.axis_index("tm"), lax.axis_index("height"), lax.axis_index("mp")
    x, i = tm // 4, lax.rem(tm, 4)
    p, c = i // 2, lax.rem(i, 2)

    up = (tm, lax.rem(h + 1, 16), m)
    down = (tm, lax.rem(h + 15, 16), m)
    ring = 2 * x + c

    def on_ring(n):
        n = lax.rem(n + 8, 8)
        return ((n // 2) * 4 + 2 * p + lax.rem(n, 2), h, m)

    left, right = on_ring(ring - 1), on_ring(ring + 1)
    sibling = (tm + 1 - 2 * c, h, m)
    across = [(lax.rem(x + d, 4) * 4 + i, h, m) for d in (1, 2, 3)]
    homes = [(4 * x + 2 * j + p, h, 1 - m) for j in range(2)]
    outside = on_ring(ring - 1 + 2 * c)

    barrier = pltpu.get_barrier_semaphore()
    partners = [
        (4 * x + lax.rem(i + di, 4), h, lax.rem(m + dm, 2))
        for di in range(4) for dm in range(2) if (di, dm) != (0, 0)
    ] + [up, down, outside] + across
    for who in partners:
        pl.semaphore_signal(barrier, inc=1, device_id=who, device_id_type=MESH)

    for dz in range(3):
        for dt in range(3):
            frame, row = tm + dt - 1, h + dz - 1
            ident = frame * 16 + row
            hit = jnp.int32(0)
            for e in range(9):
                hit = hit | jnp.where(lists[0, 0, e] == ident, 1, 0)
            inside = (frame >= 0) & (frame < 16) & (row >= 0) & (row < 16)
            hit = jnp.where(inside, hit, 0)
            bias = jnp.where(hit > 0, jnp.float32(0.0), jnp.float32(FAR))
            n = dz * 3 + dt
            mine[n:n + 1, :] = jnp.full((1, HD), bias, jnp.float32)

    pl.semaphore_wait(barrier, len(partners))

    def remote(src, dst, send, recv, who):
        return pltpu.make_async_remote_copy(
            src_ref=src, dst_ref=dst, send_sem=send, recv_sem=recv, device_id=who, device_id_type=MESH
        )

    sent = []

    def start(copy):
        copy.start()
        sent.append(copy)

    sources = (k_in, v_in, q_in)

    def tile_slot(kind, hh, slot):
        if kind == 2:
            return qbuf.at[hh, slot]
        return (kbuf, vbuf)[kind].at[hh, 1, pl.ds(pl.multiple_of((1 + slot) * TOK, TOK), TOK), :]

    def y_copy(kind, hh, j, slot, recv_slot):
        return remote(
            sources[kind].at[0, 0, :, pl.ds((3 * j + hh) * HD, HD)],
            tile_slot(kind, hh, slot), ys.at[j, kind, hh], yr.at[recv_slot, kind, hh], homes[j],
        )

    own_rows = pl.ds(pl.multiple_of(PIECE * c, 16), PIECE)
    own_cols = pl.ds(pl.multiple_of(COLS * x, COLS), COLS)

    for hh in range(G):
        for kind in range(3):
            for j in range(2):
                start(y_copy(kind, hh, j, c, c))
        if hh == 0:
            for j in range(2):
                start(remote(mine, flags.at[c], fs.at[j], fr.at[c], homes[j]))

    def w_place(z):
        return wbuf.at[x, lax.rem(z + 32, 16), c]

    for way, who in ((0, up), (1, down)):
        start(remote(w_in.at[own_rows, own_cols], w_place(h), wzs.at[way, 0], wzr.at[way, 0], who))
    local = []
    for xp in range(4):
        local.append(pltpu.make_async_copy(
            w_in.at[own_rows, pl.ds(xp * COLS, COLS)], wbuf.at[xp, h, c], ls.at[xp]))
    local.append(pltpu.make_async_copy(stream_in.at[0, 0], stream, ls.at[4]))
    for copy in local:
        copy.start()

    def w_step(k):
        for way, who in ((0, up), (1, down)):
            if way == 1 and k == 8:
                continue
            z = h - k if way == 0 else h + k
            place = w_place(z)
            remote(place, place, wzs.at[way, k - 1], wzr.at[way, k - 1], who).wait_recv()
            if k < (8 if way == 0 else 7):
                start(remote(place, place, wzs.at[way, k], wzr.at[way, k], who))
            n = way * 8 + k - 1
            for d in range(3):
                start(remote(place, place, wxs.at[d, n], wxr.at[d, n], across[d]))

    def w_share():
        for xp in range(4):
            local[xp].wait()
        for d in range(3):
            src_x = lax.rem(x + 4 - (d + 1), 4)
            for n in range(15):
                z = h - (n + 1) if n < 8 else h + (n - 7)
                place = wbuf.at[src_x, lax.rem(z + 32, 16), c]
                remote(place, place, wxs.at[d, n], wxr.at[d, n], across[d]).wait_recv()
        for xp in range(4):
            start(remote(wbuf.at[xp, :, c], wbuf.at[xp, :, c], wss.at[xp], wsr.at[xp], sibling))

    def w_shared():
        for xp in range(4):
            remote(wbuf.at[xp, :, 1 - c], wbuf.at[xp, :, 1 - c], wss.at[xp], wsr.at[xp], sibling).wait_recv()

    def edge(kind, hh, r, col):
        return (kbuf, vbuf)[kind].at[hh, r, col * TOK:(col + 1) * TOK, :]

    def q_start(kind, hh, r):
        start(remote(edge(kind, hh, r, 2), edge(kind, hh, r, 0), qs.at[0, kind, hh, r], qr.at[0, kind, hh, r], right))
        start(remote(edge(kind, hh, r, 1), edge(kind, hh, r, 3), qs.at[1, kind, hh, r], qr.at[1, kind, hh, r], left))

    def q_wait(hh):
        for kind in range(2):
            for r in range(3):
                for way, col in ((0, 0), (1, 3)):
                    ref = edge(kind, hh, r, col)
                    remote(ref, ref, qs.at[way, kind, hh, r], qr.at[way, kind, hh, r], right).wait_recv()

    def pair(kind, hh, r):
        return (kbuf, vbuf)[kind].at[hh, r, TOK:3 * TOK, :]

    def own_ready(hh):
        for kind in range(2):
            for slot in range(2):
                y_copy(kind, hh, 0, slot, slot).wait_recv()
            for way, who in ((0, up), (1, down)):
                start(remote(pair(kind, hh, 1), pair(kind, hh, 2 * way),
                             zs.at[way, kind, hh], zr.at[way, kind, hh], who))
            q_start(kind, hh, 1)

    def rows_ready(hh):
        for kind in range(2):
            for way in range(2):
                ref = pair(kind, hh, 2 * way)
                remote(ref, ref, zs.at[way, kind, hh], zr.at[way, kind, hh], up).wait_recv()
                q_start(kind, hh, 2 * way)

    def queries_ready(hh):
        for slot in range(2):
            y_copy(2, hh, 0, slot, slot).wait_recv()
            if hh == 0:
                remote(mine, flags.at[slot], fs.at[0], fr.at[slot], homes[0]).wait_recv()

    group = 2 * (1 - m) + p

    def o_copies(hh, j, mm):
        who = (4 * x + 2 * c + j, h, jnp.int32(mm))
        here = (p == c) & (c == j) & (m == mm)
        dst = oall.at[hh, :, pl.ds(pl.multiple_of(group * HD, HD), HD)]
        src = osend.at[hh, j]
        far = remote(src, dst, os_.at[j, mm, hh], or_.at[group, hh], who)
        near = pltpu.make_async_copy(src, dst, or_.at[group, hh])
        return here, far, near

    def o_start(hh):
        for j in range(2):
            for mm in range(2):
                here, far, near = o_copies(hh, j, mm)
                pl.when(here)(near.start)
                pl.when(jnp.logical_not(here))(far.start)

    def o_wait(hh):
        for g in range(4):
            dst = oall.at[hh, :, g * HD:(g + 1) * HD]
            remote(dst, dst, os_.at[0, 0, hh], or_.at[g, hh], up).wait_recv()

    own_ready(0)
    w_step(1)
    own_ready(1)
    w_step(2)
    rows_ready(0)
    w_step(3)
    queries_ready(0)
    q_wait(0)
    attend(0, qbuf, kbuf, vbuf, flags, osend)
    o_start(0)
    own_ready(2)
    w_step(4)
    w_step(5)
    rows_ready(1)
    w_step(6)
    queries_ready(1)
    q_wait(1)
    attend(1, qbuf, kbuf, vbuf, flags, osend)
    o_start(1)
    w_step(7)
    w_step(8)
    rows_ready(2)
    queries_ready(2)
    w_share()
    q_wait(2)
    attend(2, qbuf, kbuf, vbuf, flags, osend)
    o_start(2)
    w_shared()
    for hh in range(G):
        o_wait(hh)
        project(hh, oall, wbuf, acc)
    local[4].wait()
    finish(acc, stream, gate, out)

    for copy in sent:
        copy.wait_send()
    for hh in range(G):
        for j in range(2):
            for mm in range(2):
                here, far, near = o_copies(hh, j, mm)
                pl.when(jnp.logical_not(here))(far.wait_send)


def local_call(queries, key_field, value_field, stream, gate_scale, out_weight, tile_lists):
    anywhere = pl.BlockSpec(memory_space=pl.ANY)
    vmem = pl.BlockSpec(memory_space=pltpu.VMEM)
    dma = pltpu.SemaphoreType.DMA
    return pl.pallas_call(
        kernel,
        out_shape=jax.ShapeDtypeStruct(stream.shape, jnp.bfloat16),
        in_specs=[anywhere] * 4 + [vmem, anywhere, pl.BlockSpec(memory_space=pltpu.SMEM)],
        out_specs=vmem,
        scratch_shapes=[
            pltpu.VMEM((G, 2, TOK, HD), jnp.bfloat16),
            pltpu.VMEM((G, 3, 4 * TOK, HD), jnp.bfloat16),
            pltpu.VMEM((G, 3, 4 * TOK, HD), jnp.bfloat16),
            pltpu.VMEM((16, HD), jnp.float32),
            pltpu.VMEM((2, 16, HD), jnp.float32),
            pltpu.VMEM((G, 2, TOK, HD), jnp.bfloat16),
            pltpu.VMEM((G, TOK, 4 * HD), jnp.bfloat16),
            pltpu.VMEM((4, 16, 2, PIECE, COLS), jnp.bfloat16),
            pltpu.VMEM((TOK, OUT), jnp.bfloat16),
            pltpu.VMEM((TOK, OUT), jnp.float32),
            dma((2, 3, G)), dma((2, 3, G)),
            dma((2, 2, G)), dma((2, 2, G)),
            dma((2, 2, G, 3)), dma((2, 2, G, 3)),
            dma((2, 2, G)), dma((4, G)),
            dma((2,)), dma((2,)),
            dma((2, 8)), dma((2, 8)),
            dma((3, 15)), dma((3, 15)),
            dma((4,)), dma((4,)),
            dma((5,)),
        ],
        compiler_params=pltpu.CompilerParams(
            collective_id=0, has_side_effects=True, vmem_limit_bytes=52 << 20
        ),
        name="block",
    )(queries, key_field, value_field, stream, gate_scale.reshape(1, OUT), out_weight, tile_lists)


def solution(mesh):
    placed = (
        P("tm", "height", None, "mp"),
        P("tm", "height", None, "mp"),
        P("tm", "height", None, "mp"),
        P("tm", "height", None, "mp"),
        P("mp"),
        P("height", "mp"),
        P("tm", "height", None),
    )
    return jax.shard_map(
        local_call, mesh=mesh, in_specs=placed, out_specs=P("tm", "height", None, "mp"), check_vma=False
    )
```

```python
import math

import jax
import jax.numpy as jnp
from jax import lax
from jax.experimental import pallas as pl
from jax.experimental.pallas import tpu as pltpu
from jax.sharding import PartitionSpec as P

HD = 128
TOK = 384
G = 3
HALF = 768
OUT = 1536
PIECE = 48
COLS = 768
SPAN = 384
FAR = 1e30
MESH = pl.DeviceIdType.MESH


def attend(hh, tiles, qbuf, kbuf, vbuf, flags, osend):
    scale = math.log2(math.e) / math.sqrt(HD)

    for j in tiles:
        q = qbuf[hh, j]
        window = slice(j * TOK, (j + 3) * TOK)
        bias = [jnp.broadcast_to(flags[j, n:n + 1, :], (TOK, HD)) for n in range(9)]
        scores = []
        for r in range(3):
            s = lax.dot_general(
                q, kbuf[hh, r, window, :], (((1,), (1,)), ((), ())), preferred_element_type=jnp.float32
            )
            scores += [s[:, g * HD:(g + 1) * HD] for g in range(9)]
        top = None
        for n in range(9):
            a = scores[3 * n:3 * n + 3]
            t = jnp.maximum(jnp.maximum(a[0], a[1]), a[2]) - bias[n]
            top = t if top is None else jnp.maximum(top, t)
        top = jnp.broadcast_to(jnp.max(top, axis=1, keepdims=True), (TOK, HD))
        total, acc = None, None
        for r in range(3):
            weights = []
            for n in range(3 * r, 3 * r + 3):
                shift = (top + bias[n]) * scale
                weights += [jnp.exp2(a * scale - shift) for a in scores[3 * n:3 * n + 3]]
            for w in weights:
                total = w if total is None else total + w
            part = jnp.dot(
                jnp.concatenate([w.astype(jnp.bfloat16) for w in weights], axis=1),
                vbuf[hh, r, window, :], preferred_element_type=jnp.float32,
            )
            acc = part if acc is None else acc + part
        total = jnp.broadcast_to(jnp.sum(total, axis=1, keepdims=True), (TOK, HD))
        osend[hh, j] = (acc / total).astype(jnp.bfloat16)


def weight_rows(wbuf, xp, cols, start, count):
    parts = []
    row = start
    while row < start + count:
        z, rest = divmod(row, 2 * PIECE)
        c, low = divmod(rest, PIECE)
        high = min(PIECE, low + start + count - row)
        parts.append(wbuf[xp, z, c, low:high, cols])
        row += high - low
    return jnp.concatenate(parts, axis=0)


def project(hh, oall, wbuf, acc):
    left = oall[hh]
    for n in range(OUT // SPAN):
        xp, low = divmod(n * SPAN, COLS)
        right = jnp.concatenate(
            [weight_rows(wbuf, xp, slice(low, low + SPAN), (g * G + hh) * HD, HD) for g in range(4)], axis=0
        )
        part = jnp.dot(left, right, preferred_element_type=jnp.float32)
        cols = slice(n * SPAN, (n + 1) * SPAN)
        if hh == 0:
            acc[:, cols] = part
        else:
            acc[:, cols] += part


def finish(acc, stream, gate, out):
    out[0, 0] = (stream[...].astype(jnp.float32) + gate[...].reshape(1, OUT) * acc[...]).astype(jnp.bfloat16)


def kernel(
    q_in, k_in, v_in, stream_in, gate_in, w_in, lists_in, out,
    lists, gate, qbuf, kbuf, vbuf, mine, flags, osend, oall, wbuf, stream, acc,
    ys, yr, zs, zr, qs, qr, os_, or_, fs, fr, wzs, wzr, wxs, wxr, wss, wsr, ls,
):
    tm, h, m = lax.axis_index("tm"), lax.axis_index("height"), lax.axis_index("mp")
    x, i = tm // 4, lax.rem(tm, 4)
    p, c = i // 2, lax.rem(i, 2)

    up = (tm, lax.rem(h + 1, 16), m)
    down = (tm, lax.rem(h + 15, 16), m)
    ring = 2 * x + c

    def on_ring(n):
        n = lax.rem(n + 8, 8)
        return ((n // 2) * 4 + 2 * p + lax.rem(n, 2), h, m)

    left, right = on_ring(ring - 1), on_ring(ring + 1)
    sibling = (tm + 1 - 2 * c, h, m)
    across = (lax.rem(x + 1 + 2 * c, 4) * 4 + i, h, m)
    back = (lax.rem(x + 3 - 2 * c, 4) * 4 + i, h, m)
    half = lax.rem(x, 2)
    homes = [(4 * x + 2 * j + p, h, 1 - m) for j in range(2)]
    outside = on_ring(ring - 1 + 2 * c)

    barrier = pltpu.get_barrier_semaphore()
    partners = [
        (4 * x + lax.rem(i + di, 4), h, lax.rem(m + dm, 2))
        for di in range(4) for dm in range(2) if (di, dm) != (0, 0)
    ] + [up, down, outside, across, back]
    for who in partners:
        pl.semaphore_signal(barrier, inc=1, device_id=who, device_id_type=MESH)

    named = pltpu.make_async_copy(lists_in, lists, ls.at[3])
    named.start()
    gates = pltpu.make_async_copy(gate_in, gate, ls.at[4])
    gates.start()
    named.wait()

    for dz in range(3):
        for dt in range(3):
            frame, row = tm + dt - 1, h + dz - 1
            ident = frame * 16 + row
            hit = jnp.int32(0)
            for e in range(9):
                hit = hit | jnp.where(lists[0, 0, e] == ident, 1, 0)
            inside = (frame >= 0) & (frame < 16) & (row >= 0) & (row < 16)
            hit = jnp.where(inside, hit, 0)
            bias = jnp.where(hit > 0, jnp.float32(0.0), jnp.float32(FAR))
            n = dz * 3 + dt
            mine[n:n + 1, :] = jnp.full((1, HD), bias, jnp.float32)

    pl.semaphore_wait(barrier, len(partners))

    def remote(src, dst, send, recv, who):
        return pltpu.make_async_remote_copy(
            src_ref=src, dst_ref=dst, send_sem=send, recv_sem=recv, device_id=who, device_id_type=MESH
        )

    sent = []

    def start(copy):
        copy.start()
        sent.append(copy)

    sources = (k_in, v_in, q_in)

    def tile_slot(kind, hh, slot):
        if kind == 2:
            return qbuf.at[hh, slot]
        return (kbuf, vbuf)[kind].at[hh, 1, pl.ds(pl.multiple_of((1 + slot) * TOK, TOK), TOK), :]

    def y_copy(kind, hh, j, slot, recv_slot):
        return remote(
            sources[kind].at[0, 0, :, pl.ds((3 * j + hh) * HD, HD)],
            tile_slot(kind, hh, slot), ys.at[j, kind, hh], yr.at[recv_slot, kind, hh], homes[j],
        )

    own_rows = pl.ds(pl.multiple_of(PIECE * c, 16), PIECE)
    own_cols = pl.ds(pl.multiple_of(COLS * half, COLS), COLS)

    for hh in range(G):
        for kind in range(3):
            for j in range(2):
                start(y_copy(kind, hh, j, c, c))
        if hh == 0:
            for j in range(2):
                start(remote(mine, flags.at[c], fs.at[j], fr.at[c], homes[j]))

    def w_place(z):
        return wbuf.at[half, lax.rem(z + 32, 16), c]

    for way, who in ((0, up), (1, down)):
        start(remote(w_in.at[own_rows, own_cols], w_place(h), wzs.at[way, 0], wzr.at[way, 0], who))
    local = []
    for xp in range(2):
        local.append(pltpu.make_async_copy(
            w_in.at[own_rows, pl.ds(xp * COLS, COLS)], wbuf.at[xp, h, c], ls.at[xp]))
    local.append(pltpu.make_async_copy(stream_in.at[0, 0], stream, ls.at[2]))
    for copy in local:
        copy.start()

    def w_step(k):
        for way, who in ((0, up), (1, down)):
            if way == 1 and k == 8:
                continue
            z = h - k if way == 0 else h + k
            place = w_place(z)
            remote(place, place, wzs.at[way, k - 1], wzr.at[way, k - 1], who).wait_recv()
            if k < (8 if way == 0 else 7):
                start(remote(place, place, wzs.at[way, k], wzr.at[way, k], who))
            n = way * 8 + k - 1
            start(remote(place, place, wxs.at[n], wxr.at[n], across))

    def share_own():
        for xp in range(2):
            local[xp].wait()
        place = wbuf.at[half, :, c]
        start(remote(place, place, wss.at[0], wsr.at[0], sibling))

    def share_other():
        for n in range(15):
            z = h - (n + 1) if n < 8 else h + (n - 7)
            place = wbuf.at[1 - half, lax.rem(z + 32, 16), c]
            remote(place, place, wxs.at[n], wxr.at[n], across).wait_recv()
        place = wbuf.at[1 - half, :, c]
        start(remote(place, place, wss.at[1], wsr.at[1], sibling))

    def w_shared():
        for n, which in ((0, half), (1, 1 - half)):
            place = wbuf.at[which, :, 1 - c]
            remote(place, place, wss.at[n], wsr.at[n], sibling).wait_recv()

    def edge(kind, hh, r, col):
        return (kbuf, vbuf)[kind].at[hh, r, col * TOK:(col + 1) * TOK, :]

    def q_start(kind, hh, r, slot):
        if slot == 1:
            start(remote(edge(kind, hh, r, 2), edge(kind, hh, r, 0), qs.at[0, kind, hh, r], qr.at[0, kind, hh, r], right))
        else:
            start(remote(edge(kind, hh, r, 1), edge(kind, hh, r, 3), qs.at[1, kind, hh, r], qr.at[1, kind, hh, r], left))

    def q_wait(hh):
        for kind in range(2):
            for r in range(3):
                for way, col in ((0, 0), (1, 3)):
                    ref = edge(kind, hh, r, col)
                    remote(ref, ref, qs.at[way, kind, hh, r], qr.at[way, kind, hh, r], right).wait_recv()

    def own_ready(hh, kind):
        for slot in range(2):
            y_copy(kind, hh, 0, slot, slot).wait_recv()

    def z_start(hh, kind, slot):
        for way, who in ((0, up), (1, down)):
            start(remote(edge(kind, hh, 1, 1 + slot), edge(kind, hh, 2 * way, 1 + slot),
                         zs.at[way, kind, hh, slot], zr.at[way, kind, hh, slot], who))
        q_start(kind, hh, 1, slot)

    def z_pass(hh, kind, slot):
        for way in range(2):
            ref = edge(kind, hh, 2 * way, 1 + slot)
            remote(ref, ref, zs.at[way, kind, hh, slot], zr.at[way, kind, hh, slot], up).wait_recv()
            q_start(kind, hh, 2 * way, slot)

    def queries_ready(hh):
        for slot in range(2):
            y_copy(2, hh, 0, slot, slot).wait_recv()
            if hh == 0:
                remote(mine, flags.at[slot], fs.at[0], fr.at[slot], homes[0]).wait_recv()

    group = 2 * (1 - m) + p

    def o_copies(hh, j, mm):
        who = (4 * x + 2 * c + j, h, jnp.int32(mm))
        here = (p == c) & (c == j) & (m == mm)
        dst = oall.at[hh, :, pl.ds(pl.multiple_of(group * HD, HD), HD)]
        src = osend.at[hh, j]
        far = remote(src, dst, os_.at[j, mm, hh], or_.at[group, hh], who)
        near = pltpu.make_async_copy(src, dst, or_.at[group, hh])
        return here, far, near

    def o_start(hh, tiles=(0, 1)):
        for j in tiles:
            for mm in range(2):
                here, far, near = o_copies(hh, j, mm)
                pl.when(here)(near.start)
                pl.when(jnp.logical_not(here))(far.start)

    def o_wait(hh):
        for g in range(4):
            dst = oall.at[hh, :, g * HD:(g + 1) * HD]
            remote(dst, dst, os_.at[0, 0, hh], or_.at[g, hh], up).wait_recv()

    def work(hh, tiles):
        attend(hh, tiles, qbuf, kbuf, vbuf, flags, osend)
        o_start(hh, tiles)

    def chunk(n):
        return n // 4, n // 2 % 2, n % 2

    def z_next(n):
        hh, kind, slot = chunk(n)
        if slot == 0:
            own_ready(hh, kind)
        z_start(hh, kind, slot)

    w_step(1)
    for n in range(6):
        z_next(n)
        w_step(n + 2)
        if n >= 2:
            z_pass(*chunk(n - 2))
    z_next(6)
    z_next(7)
    queries_ready(0)
    q_wait(0)
    work(0, (0, 1))
    w_step(8)
    z_pass(*chunk(4))
    z_next(8)
    z_next(9)
    share_own()
    z_pass(*chunk(5))
    z_next(10)
    z_next(11)
    z_pass(*chunk(6))
    z_pass(*chunk(7))
    queries_ready(1)
    q_wait(1)
    work(1, (0, 1))
    for n in range(8, 12):
        z_pass(*chunk(n))
    queries_ready(2)
    share_other()
    q_wait(2)
    work(2, (0,))
    work(2, (1,))
    w_shared()
    for hh in range(G):
        o_wait(hh)
        project(hh, oall, wbuf, acc)
    local[2].wait()
    gates.wait()
    finish(acc, stream, gate, out)

    for copy in sent:
        copy.wait_send()
    for hh in range(G):
        for j in range(2):
            for mm in range(2):
                here, far, near = o_copies(hh, j, mm)
                pl.when(jnp.logical_not(here))(far.wait_send)


def local_call(queries, key_field, value_field, stream, gate_scale, out_weight, tile_lists):
    hbm = pl.BlockSpec(memory_space=pltpu.HBM)
    vmem = pl.BlockSpec(memory_space=pltpu.VMEM)
    dma = pltpu.SemaphoreType.DMA
    return pl.pallas_call(
        kernel,
        out_shape=jax.ShapeDtypeStruct(stream.shape, jnp.bfloat16),
        in_specs=[hbm] * 7,
        out_specs=vmem,
        scratch_shapes=[
            pltpu.SMEM((1, 1, 9), jnp.int32),
            pltpu.VMEM((OUT,), jnp.float32),
            pltpu.VMEM((G, 2, TOK, HD), jnp.bfloat16),
            pltpu.VMEM((G, 3, 4 * TOK, HD), jnp.bfloat16),
            pltpu.VMEM((G, 3, 4 * TOK, HD), jnp.bfloat16),
            pltpu.VMEM((16, HD), jnp.float32),
            pltpu.VMEM((2, 16, HD), jnp.float32),
            pltpu.VMEM((G, 2, TOK, HD), jnp.bfloat16),
            pltpu.VMEM((G, TOK, 4 * HD), jnp.bfloat16),
            pltpu.VMEM((2, 16, 2, PIECE, COLS), jnp.bfloat16),
            pltpu.VMEM((TOK, OUT), jnp.bfloat16),
            pltpu.VMEM((TOK, OUT), jnp.float32),
            dma((2, 3, G)), dma((2, 3, G)),
            dma((2, 2, G, 2)), dma((2, 2, G, 2)),
            dma((2, 2, G, 3)), dma((2, 2, G, 3)),
            dma((2, 2, G)), dma((4, G)),
            dma((2,)), dma((2,)),
            dma((2, 8)), dma((2, 8)),
            dma((15,)), dma((15,)),
            dma((2,)), dma((2,)),
            dma((5,)),
        ],
        compiler_params=pltpu.CompilerParams(
            collective_id=0, has_side_effects=True, vmem_limit_bytes=63 << 20
        ),
        name="block",
    )(queries, key_field, value_field, stream, gate_scale, out_weight, tile_lists)


def solution(mesh):
    placed = (
        P("tm", "height", None, "mp"),
        P("tm", "height", None, "mp"),
        P("tm", "height", None, "mp"),
        P("tm", "height", None, "mp"),
        P("mp"),
        P("height", "mp"),
        P("tm", "height", None),
    )
    return jax.shard_map(
        local_call, mesh=mesh, in_specs=placed, out_specs=P("tm", "height", None, "mp"), check_vma=False
    )
```

```python
import math

import jax
import jax.numpy as jnp
from jax import lax
from jax.experimental import pallas as pl
from jax.experimental.pallas import tpu as pltpu
from jax.sharding import PartitionSpec as P

HD = 128
TOK = 384
G = 3
HALF = 768
OUT = 1536
PIECE = 48
COLS = 768
SPAN = 384
FAR = 1e30
MESH = pl.DeviceIdType.MESH


def attend(hh, tiles, qbuf, kbuf, vbuf, flags, osend):
    scale = math.log2(math.e) / math.sqrt(HD)

    for j in tiles:
        q = qbuf[hh, j]
        window = slice(j * TOK, (j + 3) * TOK)
        bias = [jnp.broadcast_to(flags[j, n:n + 1, :], (TOK, HD)) for n in range(9)]
        scores = []
        for r in range(3):
            s = lax.dot_general(
                q, kbuf[hh, r, window, :], (((1,), (1,)), ((), ())), preferred_element_type=jnp.float32
            )
            scores += [s[:, g * HD:(g + 1) * HD] for g in range(9)]
        top = None
        for n in range(9):
            a = scores[3 * n:3 * n + 3]
            t = jnp.maximum(jnp.maximum(a[0], a[1]), a[2]) - bias[n]
            top = t if top is None else jnp.maximum(top, t)
        top = jnp.broadcast_to(jnp.max(top, axis=1, keepdims=True), (TOK, HD))
        total, acc = None, None
        for r in range(3):
            weights = []
            for n in range(3 * r, 3 * r + 3):
                shift = (top + bias[n]) * scale
                weights += [jnp.exp2(a * scale - shift) for a in scores[3 * n:3 * n + 3]]
            for w in weights:
                total = w if total is None else total + w
            part = jnp.dot(
                jnp.concatenate([w.astype(jnp.bfloat16) for w in weights], axis=1),
                vbuf[hh, r, window, :], preferred_element_type=jnp.float32,
            )
            acc = part if acc is None else acc + part
        total = jnp.broadcast_to(jnp.sum(total, axis=1, keepdims=True), (TOK, HD))
        osend[hh, j] = (acc / total).astype(jnp.bfloat16)


def weight_rows(wbuf, xp, cols, start, count):
    parts = []
    row = start
    while row < start + count:
        z, rest = divmod(row, 2 * PIECE)
        c, low = divmod(rest, PIECE)
        high = min(PIECE, low + start + count - row)
        parts.append(wbuf[xp, z, c, low:high, cols])
        row += high - low
    return jnp.concatenate(parts, axis=0)


def project(heads, oall, wbuf, n):
    xp, low = divmod(n * SPAN, COLS)
    left = jnp.concatenate([oall[hh] for hh in heads], axis=1)
    right = jnp.concatenate(
        [
            weight_rows(wbuf, xp, slice(low, low + SPAN), (g * G + hh) * HD, HD)
            for hh in heads for g in range(4)
        ], axis=0
    )
    return jnp.dot(left, right, preferred_element_type=jnp.float32)


def kernel(
    q_in, k_in, v_in, stream_in, gate_in, w_in, lists_in, out,
    lists, gate, qbuf, kbuf, vbuf, mine, flags, osend, oall, wbuf, stream, acc, result,
    ys, yr, zs, zr, qs, qr, os_, or_, fs, fr, wzs, wzr, wxs, wxr, wss, wsr, ls, rs,
):
    tm, h, m = lax.axis_index("tm"), lax.axis_index("height"), lax.axis_index("mp")
    x, i = tm // 4, lax.rem(tm, 4)
    p, c = i // 2, lax.rem(i, 2)

    up = (tm, lax.rem(h + 1, 16), m)
    down = (tm, lax.rem(h + 15, 16), m)
    ring = 2 * x + c

    def on_ring(n):
        n = lax.rem(n + 8, 8)
        return ((n // 2) * 4 + 2 * p + lax.rem(n, 2), h, m)

    left, right = on_ring(ring - 1), on_ring(ring + 1)
    sibling = (tm + 1 - 2 * c, h, m)
    across = (lax.rem(x + 1 + 2 * c, 4) * 4 + i, h, m)
    back = (lax.rem(x + 3 - 2 * c, 4) * 4 + i, h, m)
    half = lax.rem(x, 2)
    homes = [(4 * x + 2 * j + p, h, 1 - m) for j in range(2)]
    outside = on_ring(ring - 1 + 2 * c)

    barrier = pltpu.get_barrier_semaphore()
    partners = [
        (4 * x + lax.rem(i + di, 4), h, lax.rem(m + dm, 2))
        for di in range(4) for dm in range(2) if (di, dm) != (0, 0)
    ] + [up, down, outside, across, back]
    for who in partners:
        pl.semaphore_signal(barrier, inc=1, device_id=who, device_id_type=MESH)

    named = pltpu.make_async_copy(lists_in, lists, ls.at[3])
    named.start()
    gates = pltpu.make_async_copy(gate_in, gate, ls.at[4])
    gates.start()
    named.wait()

    for dz in range(3):
        for dt in range(3):
            frame, row = tm + dt - 1, h + dz - 1
            ident = frame * 16 + row
            hit = jnp.int32(0)
            for e in range(9):
                hit = hit | jnp.where(lists[0, 0, e] == ident, 1, 0)
            inside = (frame >= 0) & (frame < 16) & (row >= 0) & (row < 16)
            hit = jnp.where(inside, hit, 0)
            bias = jnp.where(hit > 0, jnp.float32(0.0), jnp.float32(FAR))
            n = dz * 3 + dt
            mine[n:n + 1, :] = jnp.full((1, HD), bias, jnp.float32)

    pl.semaphore_wait(barrier, len(partners))

    def remote(src, dst, send, recv, who):
        return pltpu.make_async_remote_copy(
            src_ref=src, dst_ref=dst, send_sem=send, recv_sem=recv, device_id=who, device_id_type=MESH
        )

    sent = []

    def start(copy):
        copy.start()
        sent.append(copy)

    sources = (k_in, v_in, q_in)

    def tile_slot(kind, hh, slot):
        if kind == 2:
            return qbuf.at[hh, slot]
        return (kbuf, vbuf)[kind].at[hh, 1, pl.ds(pl.multiple_of((1 + slot) * TOK, TOK), TOK), :]

    def y_copy(kind, hh, j, slot, recv_slot):
        return remote(
            sources[kind].at[0, 0, :, pl.ds((3 * j + hh) * HD, HD)],
            tile_slot(kind, hh, slot), ys.at[j, kind, hh], yr.at[recv_slot, kind, hh], homes[j],
        )

    own_rows = pl.ds(pl.multiple_of(PIECE * c, 16), PIECE)
    own_cols = pl.ds(pl.multiple_of(COLS * half, COLS), COLS)

    for hh in range(G):
        for kind in range(3):
            for j in range(2):
                start(y_copy(kind, hh, j, c, c))
        if hh == 0:
            for j in range(2):
                start(remote(mine, flags.at[c], fs.at[j], fr.at[c], homes[j]))

    def w_place(z):
        return wbuf.at[half, lax.rem(z + 32, 16), c]

    for way, who in ((0, up), (1, down)):
        start(remote(w_in.at[own_rows, own_cols], w_place(h), wzs.at[way, 0], wzr.at[way, 0], who))
    local = []
    for xp in range(2):
        local.append(pltpu.make_async_copy(
            w_in.at[own_rows, pl.ds(xp * COLS, COLS)], wbuf.at[xp, h, c], ls.at[xp]))
    local.append(pltpu.make_async_copy(stream_in.at[0, 0], stream, ls.at[2]))
    for copy in local:
        copy.start()

    def w_step(k):
        for way, who in ((0, up), (1, down)):
            if way == 1 and k == 8:
                continue
            z = h - k if way == 0 else h + k
            place = w_place(z)
            remote(place, place, wzs.at[way, k - 1], wzr.at[way, k - 1], who).wait_recv()
            if k < (8 if way == 0 else 7):
                start(remote(place, place, wzs.at[way, k], wzr.at[way, k], who))
            n = way * 8 + k - 1
            start(remote(place, place, wxs.at[n], wxr.at[n], across))

    def share_own():
        for xp in range(2):
            local[xp].wait()
        place = wbuf.at[half, :, c]
        start(remote(place, place, wss.at[0], wsr.at[0], sibling))

    def share_other():
        for n in range(15):
            z = h - (n + 1) if n < 8 else h + (n - 7)
            place = wbuf.at[1 - half, lax.rem(z + 32, 16), c]
            remote(place, place, wxs.at[n], wxr.at[n], across).wait_recv()
        place = wbuf.at[1 - half, :, c]
        start(remote(place, place, wss.at[1], wsr.at[1], sibling))

    def w_shared():
        for n, which in ((0, half), (1, 1 - half)):
            place = wbuf.at[which, :, 1 - c]
            remote(place, place, wss.at[n], wsr.at[n], sibling).wait_recv()

    def edge(kind, hh, r, col):
        return (kbuf, vbuf)[kind].at[hh, r, col * TOK:(col + 1) * TOK, :]

    def q_start(kind, hh, r, slot):
        if slot == 1:
            start(remote(edge(kind, hh, r, 2), edge(kind, hh, r, 0), qs.at[0, kind, hh, r], qr.at[0, kind, hh, r], right))
        else:
            start(remote(edge(kind, hh, r, 1), edge(kind, hh, r, 3), qs.at[1, kind, hh, r], qr.at[1, kind, hh, r], left))

    def q_wait(hh):
        for kind in range(2):
            for r in range(3):
                for way, col in ((0, 0), (1, 3)):
                    ref = edge(kind, hh, r, col)
                    remote(ref, ref, qs.at[way, kind, hh, r], qr.at[way, kind, hh, r], right).wait_recv()

    def own_ready(hh, kind):
        for slot in range(2):
            y_copy(kind, hh, 0, slot, slot).wait_recv()

    def z_start(hh, kind, slot):
        for way, who in ((0, up), (1, down)):
            start(remote(edge(kind, hh, 1, 1 + slot), edge(kind, hh, 2 * way, 1 + slot),
                         zs.at[way, kind, hh, slot], zr.at[way, kind, hh, slot], who))
        q_start(kind, hh, 1, slot)

    def z_pass(hh, kind, slot):
        for way in range(2):
            ref = edge(kind, hh, 2 * way, 1 + slot)
            remote(ref, ref, zs.at[way, kind, hh, slot], zr.at[way, kind, hh, slot], up).wait_recv()
            q_start(kind, hh, 2 * way, slot)

    def queries_ready(hh):
        for slot in range(2):
            y_copy(2, hh, 0, slot, slot).wait_recv()
            if hh == 0:
                remote(mine, flags.at[slot], fs.at[0], fr.at[slot], homes[0]).wait_recv()

    group = 2 * (1 - m) + p

    def o_copies(hh, j, mm):
        who = (4 * x + 2 * c + j, h, jnp.int32(mm))
        here = (p == c) & (c == j) & (m == mm)
        dst = oall.at[hh, :, pl.ds(pl.multiple_of(group * HD, HD), HD)]
        src = osend.at[hh, j]
        far = remote(src, dst, os_.at[j, mm, hh], or_.at[group, hh], who)
        near = pltpu.make_async_copy(src, dst, or_.at[group, hh])
        return here, far, near

    def o_start(hh, tiles=(0, 1)):
        for j in tiles:
            for mm in range(2):
                here, far, near = o_copies(hh, j, mm)
                pl.when(here)(near.start)
                pl.when(jnp.logical_not(here))(far.start)

    def o_wait(hh):
        for g in range(4):
            dst = oall.at[hh, :, g * HD:(g + 1) * HD]
            remote(dst, dst, os_.at[0, 0, hh], or_.at[g, hh], up).wait_recv()

    def work(hh, tiles):
        attend(hh, tiles, qbuf, kbuf, vbuf, flags, osend)
        o_start(hh, tiles)

    def chunk(n):
        return n // 4, n // 2 % 2, n % 2

    def z_next(n):
        hh, kind, slot = chunk(n)
        if slot == 0:
            own_ready(hh, kind)
        z_start(hh, kind, slot)

    w_step(1)
    z_next(0)
    z_next(1)
    w_step(2)
    z_next(2)
    z_next(3)
    w_step(3)
    z_pass(*chunk(0))
    z_pass(*chunk(1))
    z_next(4)
    z_next(5)
    w_step(4)
    z_pass(*chunk(2))
    z_pass(*chunk(3))
    z_next(6)
    z_next(7)
    w_step(5)
    z_pass(*chunk(4))
    z_pass(*chunk(5))
    z_next(8)
    z_next(9)
    queries_ready(0)
    q_wait(0)
    work(0, (0, 1))
    w_step(6)
    z_pass(*chunk(6))
    z_pass(*chunk(7))
    z_next(10)
    z_next(11)
    w_step(7)
    queries_ready(1)
    q_wait(1)
    work(1, (0, 1))
    z_pass(*chunk(8))
    z_pass(*chunk(9))
    w_step(8)
    share_own()
    z_pass(*chunk(10))
    z_pass(*chunk(11))
    share_other()
    queries_ready(2)
    q_wait(2)
    work(2, (0,))
    work(2, (1,))
    w_shared()
    o_wait(0)
    o_wait(1)
    for n in range(OUT // SPAN):
        acc[:, n * SPAN:(n + 1) * SPAN] = project((0, 1), oall, wbuf, n)
    local[2].wait()
    gates.wait()
    o_wait(2)
    leaving = []
    for n in range(OUT // SPAN):
        cols = slice(n * SPAN, (n + 1) * SPAN)
        mixed = acc[:, cols] + project((2,), oall, wbuf, n)
        result[:, cols] = (
            stream[:, cols].astype(jnp.float32) + gate[cols].reshape(1, SPAN) * mixed
        ).astype(jnp.bfloat16)
        copy = pltpu.make_async_copy(result.at[:, cols], out.at[0, 0, :, cols], rs.at[n])
        copy.start()
        leaving.append(copy)
    for copy in leaving:
        copy.wait()

    for copy in sent:
        copy.wait_send()
    for hh in range(G):
        for j in range(2):
            for mm in range(2):
                here, far, near = o_copies(hh, j, mm)
                pl.when(jnp.logical_not(here))(far.wait_send)


def local_call(queries, key_field, value_field, stream, gate_scale, out_weight, tile_lists):
    hbm = pl.BlockSpec(memory_space=pltpu.HBM)
    dma = pltpu.SemaphoreType.DMA
    return pl.pallas_call(
        kernel,
        out_shape=jax.ShapeDtypeStruct(stream.shape, jnp.bfloat16),
        in_specs=[hbm] * 7,
        out_specs=hbm,
        scratch_shapes=[
            pltpu.SMEM((1, 1, 9), jnp.int32),
            pltpu.VMEM((OUT,), jnp.float32),
            pltpu.VMEM((G, 2, TOK, HD), jnp.bfloat16),
            pltpu.VMEM((G, 3, 4 * TOK, HD), jnp.bfloat16),
            pltpu.VMEM((G, 3, 4 * TOK, HD), jnp.bfloat16),
            pltpu.VMEM((16, HD), jnp.float32),
            pltpu.VMEM((2, 16, HD), jnp.float32),
            pltpu.VMEM((G, 2, TOK, HD), jnp.bfloat16),
            pltpu.VMEM((G, TOK, 4 * HD), jnp.bfloat16),
            pltpu.VMEM((2, 16, 2, PIECE, COLS), jnp.bfloat16),
            pltpu.VMEM((TOK, OUT), jnp.bfloat16),
            pltpu.VMEM((TOK, OUT), jnp.float32),
            pltpu.VMEM((TOK, OUT), jnp.bfloat16),
            dma((2, 3, G)), dma((2, 3, G)),
            dma((2, 2, G, 2)), dma((2, 2, G, 2)),
            dma((2, 2, G, 3)), dma((2, 2, G, 3)),
            dma((2, 2, G)), dma((4, G)),
            dma((2,)), dma((2,)),
            dma((2, 8)), dma((2, 8)),
            dma((15,)), dma((15,)),
            dma((2,)), dma((2,)),
            dma((5,)), dma((4,)),
        ],
        compiler_params=pltpu.CompilerParams(
            collective_id=0, has_side_effects=True, vmem_limit_bytes=63 << 20
        ),
        name="block",
    )(queries, key_field, value_field, stream, gate_scale, out_weight, tile_lists)


def solution(mesh):
    placed = (
        P("tm", "height", None, "mp"),
        P("tm", "height", None, "mp"),
        P("tm", "height", None, "mp"),
        P("tm", "height", None, "mp"),
        P("mp"),
        P("height", "mp"),
        P("tm", "height", None),
    )
    return jax.shard_map(
        local_call, mesh=mesh, in_specs=placed, out_specs=P("tm", "height", None, "mp"), check_vma=False
    )
```

```python
import math

import jax
import jax.numpy as jnp
from jax import lax
from jax.experimental import pallas as pl
from jax.experimental.pallas import tpu as pltpu
from jax.sharding import PartitionSpec as P

HD = 128
TOK = 384
G = 3
HALF = 768
OUT = 1536
PIECE = 48
COLS = 768
SPAN = 384
FAR = 1e30
MESH = pl.DeviceIdType.MESH


def attend(hh, tiles, qbuf, kbuf, vbuf, flags, osend):
    scale = math.log2(math.e) / math.sqrt(HD)

    for j in tiles:
        q = qbuf[hh, j]
        window = slice(j * TOK, (j + 3) * TOK)
        bias = [jnp.broadcast_to(flags[j, n:n + 1, :], (TOK, HD)) for n in range(9)]
        scores = []
        for r in range(3):
            s = lax.dot_general(
                q, kbuf[hh, r, window, :], (((1,), (1,)), ((), ())), preferred_element_type=jnp.float32
            )
            scores += [s[:, g * HD:(g + 1) * HD] for g in range(9)]
        top = None
        for n in range(9):
            a = scores[3 * n:3 * n + 3]
            t = jnp.maximum(jnp.maximum(a[0], a[1]), a[2]) - bias[n]
            top = t if top is None else jnp.maximum(top, t)
        top = jnp.broadcast_to(jnp.max(top, axis=1, keepdims=True), (TOK, HD))
        total, acc = None, None
        for r in range(3):
            weights = []
            for n in range(3 * r, 3 * r + 3):
                shift = (top + bias[n]) * scale
                weights += [jnp.exp2(a * scale - shift) for a in scores[3 * n:3 * n + 3]]
            for w in weights:
                total = w if total is None else total + w
            part = jnp.dot(
                jnp.concatenate([w.astype(jnp.bfloat16) for w in weights], axis=1),
                vbuf[hh, r, window, :], preferred_element_type=jnp.float32,
            )
            acc = part if acc is None else acc + part
        total = jnp.broadcast_to(jnp.sum(total, axis=1, keepdims=True), (TOK, HD))
        osend[hh, j] = (acc / total).astype(jnp.bfloat16)


def weight_rows(wbuf, xp, cols, start, count):
    parts = []
    row = start
    while row < start + count:
        z, rest = divmod(row, 2 * PIECE)
        c, low = divmod(rest, PIECE)
        high = min(PIECE, low + start + count - row)
        parts.append(wbuf[xp, z, c, low:high, cols])
        row += high - low
    return jnp.concatenate(parts, axis=0)


def project(heads, oall, wbuf, n):
    xp, low = divmod(n * SPAN, COLS)
    left = jnp.concatenate([oall[hh] for hh in heads], axis=1)
    right = jnp.concatenate(
        [
            weight_rows(wbuf, xp, slice(low, low + SPAN), (g * G + hh) * HD, HD)
            for hh in heads for g in range(4)
        ], axis=0
    )
    return jnp.dot(left, right, preferred_element_type=jnp.float32)


def kernel(
    q_in, k_in, v_in, stream_in, gate_in, w_in, lists_in, out,
    lists, gate, qbuf, kbuf, vbuf, mine, flags, osend, oall, wbuf, stream, acc, result,
    ys, yr, zs, zr, qs, qr, os_, or_, fs, fr, wzs, wzr, wxs, wxr, wss, wsr, ls, rs,
):
    tm, h, m = lax.axis_index("tm"), lax.axis_index("height"), lax.axis_index("mp")
    x, i = tm // 4, lax.rem(tm, 4)
    p, c = i // 2, lax.rem(i, 2)

    up = (tm, lax.rem(h + 1, 16), m)
    down = (tm, lax.rem(h + 15, 16), m)
    ring = 2 * x + c

    def on_ring(n):
        n = lax.rem(n + 8, 8)
        return ((n // 2) * 4 + 2 * p + lax.rem(n, 2), h, m)

    left, right = on_ring(ring - 1), on_ring(ring + 1)
    sibling = (tm + 1 - 2 * c, h, m)
    across = (lax.rem(x + 1 + 2 * c, 4) * 4 + i, h, m)
    back = (lax.rem(x + 3 - 2 * c, 4) * 4 + i, h, m)
    half = lax.rem(x, 2)
    homes = [(4 * x + 2 * j + p, h, 1 - m) for j in range(2)]
    outside = on_ring(ring - 1 + 2 * c)

    barrier = pltpu.get_barrier_semaphore()
    partners = [
        (4 * x + lax.rem(i + di, 4), h, lax.rem(m + dm, 2))
        for di in range(4) for dm in range(2) if (di, dm) != (0, 0)
    ] + [up, down, outside, across, back]
    for who in partners:
        pl.semaphore_signal(barrier, inc=1, device_id=who, device_id_type=MESH)

    named = pltpu.make_async_copy(lists_in, lists, ls.at[3])
    named.start()
    gates = pltpu.make_async_copy(gate_in, gate, ls.at[4])
    gates.start()
    named.wait()

    for dz in range(3):
        for dt in range(3):
            frame, row = tm + dt - 1, h + dz - 1
            ident = frame * 16 + row
            hit = jnp.int32(0)
            for e in range(9):
                hit = hit | jnp.where(lists[0, 0, e] == ident, 1, 0)
            inside = (frame >= 0) & (frame < 16) & (row >= 0) & (row < 16)
            hit = jnp.where(inside, hit, 0)
            bias = jnp.where(hit > 0, jnp.float32(0.0), jnp.float32(FAR))
            n = dz * 3 + dt
            mine[n:n + 1, :] = jnp.full((1, HD), bias, jnp.float32)

    pl.semaphore_wait(barrier, len(partners))

    def remote(src, dst, send, recv, who):
        return pltpu.make_async_remote_copy(
            src_ref=src, dst_ref=dst, send_sem=send, recv_sem=recv, device_id=who, device_id_type=MESH
        )

    sent = []

    def start(copy):
        copy.start()
        sent.append(copy)

    sources = (k_in, v_in, q_in)

    def tile_slot(kind, hh, slot):
        if kind == 2:
            return qbuf.at[hh, slot]
        return (kbuf, vbuf)[kind].at[hh, 1, pl.ds(pl.multiple_of((1 + slot) * TOK, TOK), TOK), :]

    def y_copy(kind, hh, j, slot, recv_slot):
        return remote(
            sources[kind].at[0, 0, :, pl.ds((3 * j + hh) * HD, HD)],
            tile_slot(kind, hh, slot), ys.at[j, kind, hh], yr.at[recv_slot, kind, hh], homes[j],
        )

    own_rows = pl.ds(pl.multiple_of(PIECE * c, 16), PIECE)
    own_cols = pl.ds(pl.multiple_of(COLS * half, COLS), COLS)

    for n, (kind, hh) in enumerate([(k, g) for g in range(G) for k in (0, 1)] + [(2, g) for g in range(G)]):
        for j in range(2):
            start(y_copy(kind, hh, j, c, c))
        if n == 1:
            for j in range(2):
                start(remote(mine, flags.at[c], fs.at[j], fr.at[c], homes[j]))

    def w_place(z):
        return wbuf.at[half, lax.rem(z + 32, 16), c]

    for way, who in ((0, up), (1, down)):
        start(remote(w_in.at[own_rows, own_cols], w_place(h), wzs.at[way, 0], wzr.at[way, 0], who))
    local = []
    for xp in range(2):
        local.append(pltpu.make_async_copy(
            w_in.at[own_rows, pl.ds(xp * COLS, COLS)], wbuf.at[xp, h, c], ls.at[xp]))
    local.append(pltpu.make_async_copy(stream_in.at[0, 0], stream, ls.at[2]))
    for copy in local:
        copy.start()

    def w_step(k):
        for way, who in ((0, up), (1, down)):
            if way == 1 and k == 8:
                continue
            z = h - k if way == 0 else h + k
            place = w_place(z)
            remote(place, place, wzs.at[way, k - 1], wzr.at[way, k - 1], who).wait_recv()
            if k < (8 if way == 0 else 7):
                start(remote(place, place, wzs.at[way, k], wzr.at[way, k], who))
            n = way * 8 + k - 1
            start(remote(place, place, wxs.at[n], wxr.at[n], across))

    def share_own():
        for xp in range(2):
            local[xp].wait()
        place = wbuf.at[half, :, c]
        start(remote(place, place, wss.at[0], wsr.at[0], sibling))

    def share_other():
        for n in range(15):
            z = h - (n + 1) if n < 8 else h + (n - 7)
            place = wbuf.at[1 - half, lax.rem(z + 32, 16), c]
            remote(place, place, wxs.at[n], wxr.at[n], across).wait_recv()
        place = wbuf.at[1 - half, :, c]
        start(remote(place, place, wss.at[1], wsr.at[1], sibling))

    def w_shared():
        for n, which in ((0, half), (1, 1 - half)):
            place = wbuf.at[which, :, 1 - c]
            remote(place, place, wss.at[n], wsr.at[n], sibling).wait_recv()

    def edge(kind, hh, r, col):
        return (kbuf, vbuf)[kind].at[hh, r, col * TOK:(col + 1) * TOK, :]

    def q_start(kind, hh, r, slot):
        if slot == 1:
            start(remote(edge(kind, hh, r, 2), edge(kind, hh, r, 0), qs.at[0, kind, hh, r], qr.at[0, kind, hh, r], right))
        else:
            start(remote(edge(kind, hh, r, 1), edge(kind, hh, r, 3), qs.at[1, kind, hh, r], qr.at[1, kind, hh, r], left))

    def q_wait(hh):
        for kind in range(2):
            for r in range(3):
                for way, col in ((0, 0), (1, 3)):
                    ref = edge(kind, hh, r, col)
                    remote(ref, ref, qs.at[way, kind, hh, r], qr.at[way, kind, hh, r], right).wait_recv()

    def own_ready(hh, kind):
        for slot in range(2):
            y_copy(kind, hh, 0, slot, slot).wait_recv()

    def z_start(hh, kind, slot):
        for way, who in ((0, up), (1, down)):
            start(remote(edge(kind, hh, 1, 1 + slot), edge(kind, hh, 2 * way, 1 + slot),
                         zs.at[way, kind, hh, slot], zr.at[way, kind, hh, slot], who))
        q_start(kind, hh, 1, slot)

    def z_pass(hh, kind, slot):
        for way in range(2):
            ref = edge(kind, hh, 2 * way, 1 + slot)
            remote(ref, ref, zs.at[way, kind, hh, slot], zr.at[way, kind, hh, slot], up).wait_recv()
            q_start(kind, hh, 2 * way, slot)

    def queries_ready(hh):
        for slot in range(2):
            y_copy(2, hh, 0, slot, slot).wait_recv()
            if hh == 0:
                remote(mine, flags.at[slot], fs.at[0], fr.at[slot], homes[0]).wait_recv()

    group = 2 * (1 - m) + p

    def o_copies(hh, j, mm):
        who = (4 * x + 2 * c + j, h, jnp.int32(mm))
        here = (p == c) & (c == j) & (m == mm)
        dst = oall.at[hh, :, pl.ds(pl.multiple_of(group * HD, HD), HD)]
        src = osend.at[hh, j]
        far = remote(src, dst, os_.at[j, mm, hh], or_.at[group, hh], who)
        near = pltpu.make_async_copy(src, dst, or_.at[group, hh])
        return here, far, near

    def o_start(hh, tiles=(0, 1)):
        for j in tiles:
            for mm in range(2):
                here, far, near = o_copies(hh, j, mm)
                pl.when(here)(near.start)
                pl.when(jnp.logical_not(here))(far.start)

    def o_wait(hh):
        for g in range(4):
            dst = oall.at[hh, :, g * HD:(g + 1) * HD]
            remote(dst, dst, os_.at[0, 0, hh], or_.at[g, hh], up).wait_recv()

    def work(hh, tiles):
        attend(hh, tiles, qbuf, kbuf, vbuf, flags, osend)
        o_start(hh, tiles)

    def chunk(n):
        return n // 4, n // 2 % 2, n % 2

    def z_next(n):
        hh, kind, slot = chunk(n)
        if slot == 0:
            own_ready(hh, kind)
        z_start(hh, kind, slot)

    w_step(1)
    z_next(0)
    z_next(1)
    w_step(2)
    z_next(2)
    z_next(3)
    w_step(3)
    z_pass(*chunk(0))
    z_pass(*chunk(1))
    z_next(4)
    z_next(5)
    w_step(4)
    z_pass(*chunk(2))
    z_pass(*chunk(3))
    z_next(6)
    z_next(7)
    w_step(5)
    z_pass(*chunk(4))
    z_pass(*chunk(5))
    z_next(8)
    z_next(9)
    queries_ready(0)
    q_wait(0)
    work(0, (0, 1))
    w_step(6)
    z_pass(*chunk(6))
    z_pass(*chunk(7))
    z_next(10)
    z_next(11)
    w_step(7)
    queries_ready(1)
    q_wait(1)
    work(1, (0, 1))
    z_pass(*chunk(8))
    z_pass(*chunk(9))
    w_step(8)
    share_own()
    z_pass(*chunk(10))
    z_pass(*chunk(11))
    share_other()
    queries_ready(2)
    q_wait(2)
    work(2, (0,))
    work(2, (1,))
    w_shared()
    o_wait(0)
    o_wait(1)
    for n in range(OUT // SPAN):
        acc[:, n * SPAN:(n + 1) * SPAN] = project((0, 1), oall, wbuf, n)
    local[2].wait()
    gates.wait()
    o_wait(2)
    leaving = []
    for n in range(OUT // SPAN):
        cols = slice(n * SPAN, (n + 1) * SPAN)
        mixed = acc[:, cols] + project((2,), oall, wbuf, n)
        result[:, cols] = (
            stream[:, cols].astype(jnp.float32) + gate[cols].reshape(1, SPAN) * mixed
        ).astype(jnp.bfloat16)
        copy = pltpu.make_async_copy(result.at[:, cols], out.at[0, 0, :, cols], rs.at[n])
        copy.start()
        leaving.append(copy)
    for copy in leaving:
        copy.wait()

    for copy in sent:
        copy.wait_send()
    for hh in range(G):
        for j in range(2):
            for mm in range(2):
                here, far, near = o_copies(hh, j, mm)
                pl.when(jnp.logical_not(here))(far.wait_send)


def local_call(queries, key_field, value_field, stream, gate_scale, out_weight, tile_lists):
    hbm = pl.BlockSpec(memory_space=pltpu.HBM)
    dma = pltpu.SemaphoreType.DMA
    return pl.pallas_call(
        kernel,
        out_shape=jax.ShapeDtypeStruct(stream.shape, jnp.bfloat16),
        in_specs=[hbm] * 7,
        out_specs=hbm,
        scratch_shapes=[
            pltpu.SMEM((1, 1, 9), jnp.int32),
            pltpu.VMEM((OUT,), jnp.float32),
            pltpu.VMEM((G, 2, TOK, HD), jnp.bfloat16),
            pltpu.VMEM((G, 3, 4 * TOK, HD), jnp.bfloat16),
            pltpu.VMEM((G, 3, 4 * TOK, HD), jnp.bfloat16),
            pltpu.VMEM((16, HD), jnp.float32),
            pltpu.VMEM((2, 16, HD), jnp.float32),
            pltpu.VMEM((G, 2, TOK, HD), jnp.bfloat16),
            pltpu.VMEM((G, TOK, 4 * HD), jnp.bfloat16),
            pltpu.VMEM((2, 16, 2, PIECE, COLS), jnp.bfloat16),
            pltpu.VMEM((TOK, OUT), jnp.bfloat16),
            pltpu.VMEM((TOK, OUT), jnp.float32),
            pltpu.VMEM((TOK, OUT), jnp.bfloat16),
            dma((2, 3, G)), dma((2, 3, G)),
            dma((2, 2, G, 2)), dma((2, 2, G, 2)),
            dma((2, 2, G, 3)), dma((2, 2, G, 3)),
            dma((2, 2, G)), dma((4, G)),
            dma((2,)), dma((2,)),
            dma((2, 8)), dma((2, 8)),
            dma((15,)), dma((15,)),
            dma((2,)), dma((2,)),
            dma((5,)), dma((4,)),
        ],
        compiler_params=pltpu.CompilerParams(
            collective_id=0, has_side_effects=True, vmem_limit_bytes=63 << 20
        ),
        name="block",
    )(queries, key_field, value_field, stream, gate_scale, out_weight, tile_lists)


def solution(mesh):
    placed = (
        P("tm", "height", None, "mp"),
        P("tm", "height", None, "mp"),
        P("tm", "height", None, "mp"),
        P("tm", "height", None, "mp"),
        P("mp"),
        P("height", "mp"),
        P("tm", "height", None),
    )
    return jax.shard_map(
        local_call, mesh=mesh, in_specs=placed, out_specs=P("tm", "height", None, "mp"), check_vma=False
    )
```
